256 devices in a mesh: blk: 32 (over y, z_hi, core), freq: 8 (over x, z_lo).
Axes of the slice: x: 4, y: 4, z: 8 (z_hi: 4, z_lo: 2; z = z_hi * 2 + z_lo), core: 2. Of those that a mesh axis runs over, the one named last changes fastest.
Arguments:
- forcing_hat: bfloat16 [2, 64, 2, 5, 2048, 128], P(None, 'freq', None, None, 'blk'), may hold values from -6 to 6
- mean_speed: float32 [2048, 128], P('blk'), may hold values from 0.2 to 0.9
- block_order: int32 [128], P('blk'), may hold values from 0 to 3, as said below
- block_flips: int32 [128], P('blk'), may hold values from 0 to 1
Outputs:
- response_hat: float32 [2, 64, 2, 5, 2048, 128], P(None, 'freq', None, None, 'blk')
The draws below stay inside these ranges and needn't reach their ends.
Inputs may be any that keep to these rules, and one draw needn't show every extreme that they name: `block_order`: each aligned group of 4 entries (the blocks of one index of blk) is a permutation of 0 to 3.
All inputs are finite; a program needn't handle non-finite values.
Results may differ from the reference program's by a relative error of at most 0.0021.
Values sent between devices are 32-bit elements; how exact they have to be, the bound alone decides.
No kernel may reach another device: no remote copies, remote signals or barrier semaphores. Data moves between devices by JAX's collectives and lax.ppermute only.
A program may use at most 64 MiB of HBM per device.

```python
import math
import jax
import jax.numpy as jnp
from jax import lax

NJ = 128
BPD = 4
K = 2
F = 64
STEPS = 8
NBLOCKS = 128
ROWS = 2048


def draw_block_order(key, part):
    scores = jax.random.randint(key, (NBLOCKS // BPD, BPD), 0, 1 << 16) * BPD + jnp.arange(BPD, dtype=jnp.int32)[None, :]
    return jnp.argsort(scores, axis=1, stable=True).astype(jnp.int32).reshape(NBLOCKS)


def set_ends(drawn, own_key, low, high):
    dims = drawn.shape
    index_at = [jax.random.randint(jax.random.fold_in(own_key, axis), (), 0, dims[axis]) for axis in range(len(dims))]
    drawn = drawn.at[tuple(index_at)].set(low)
    longest = dims.index(max(dims))
    index_at[longest] = (index_at[longest] + 1) % dims[longest]
    return drawn.at[tuple(index_at)].set(high)


def level_of(rng, shape, pieces, smallest, largest):
    def one(dim, blocks):
        heights = jax.random.uniform(jax.random.fold_in(jax.random.fold_in(rng, 6), dim), (blocks,), jnp.float32, smallest / len(pieces), largest / len(pieces))
        return jnp.repeat(jnp.exp(heights), shape[dim] // blocks).reshape((-1,) + (1,) * (len(shape) - dim - 1))

    gain = one(*pieces[0])
    for cut in pieces[1:]:
        gain = gain * one(*cut)
    return gain


def normal_values(key, shape, spread, limit, shards=(), held_as=jnp.bfloat16):
    gain = level_of(key, shape, shards, -0.22, 0.18) if shards else 1.0
    array = jax.random.normal(key, shape, jnp.float32) * spread * gain
    return jnp.minimum(jnp.maximum(array, -limit), limit).astype(held_as)


def setup_inputs(seed: int = 0) -> dict:
    arg_keys = jax.random.split(jax.random.key(seed), 5)
    forcing_hat = normal_values(arg_keys[0], (2, F, K, 5, ROWS, NJ), 1.0, 6.0, ((1, 8), (4, 32)))
    mean_speed = jnp.clip(0.2 + 0.7 * jax.random.uniform(arg_keys[1], (ROWS, NJ), jnp.float32) ** level_of(arg_keys[1], (ROWS, NJ), ((0, 32),), -0.2, 0.2), 0.2, 0.9)
    block_order = draw_block_order(jax.random.fold_in(arg_keys[4], 71), 0)
    block_flips = set_ends(jax.random.randint(arg_keys[3], (NBLOCKS,), 0, 2), jax.random.fold_in(arg_keys[3], 1), 0, 1).astype(jnp.int32)
    return {"forcing_hat": forcing_hat, "mean_speed": mean_speed, "block_order": block_order, "block_flips": block_flips}


time_step = 0.4
viscosity = 0.5

def flip_blocks(blocked, flip_flags):
    return jnp.where((flip_flags == 1)[:, None, None], blocked[..., ::-1], blocked)

def to_chain(values, chain_ids, flip_flags, block_count):
    blocked = values.reshape(values.shape[:-2] + (block_count, values.shape[-2] // block_count, values.shape[-1]))
    placed = jnp.take(blocked, chain_ids, axis=-3)
    placed = flip_blocks(placed, jnp.take(flip_flags, chain_ids))
    return placed.reshape(values.shape)

def from_chain(values, chain_ids, flip_flags, block_count):
    inverse = jnp.argsort(chain_ids).astype(jnp.int32)
    blocked = values.reshape(values.shape[:-2] + (block_count, values.shape[-2] // block_count, values.shape[-1]))
    placed = jnp.take(blocked, inverse, axis=-3)
    placed = flip_blocks(placed, flip_flags)
    return placed.reshape(values.shape)

def tendency(extended, mean_speed):
    center = extended[:, :, 1:-1, 1:-1]
    upper_row = extended[:, :, 2:, 1:-1]
    lower_row = extended[:, :, :-2, 1:-1]
    right_col = extended[:, :, 1:-1, 2:]
    left_col = extended[:, :, 1:-1, :-2]
    stream_diff = 0.5 * (upper_row - lower_row)
    cross_diff = 0.5 * (right_col - left_col)
    laplace = upper_row + lower_row + right_col + left_col - 4.0 * center
    advection = -mean_speed * stream_diff
    divergence = stream_diff[:, 1] + cross_diff[:, 2]
    rates = jnp.stack([advection[:, 0] - divergence, advection[:, 1] - stream_diff[:, 3], advection[:, 2] - cross_diff[:, 3], advection[:, 3] - divergence, advection[:, 4]], axis=1)
    return rates + viscosity * laplace

def synthesis_table(freq_ids):
    angular = (freq_ids + 1.0) * (math.pi / F)
    times = jnp.arange(STEPS, dtype=jnp.float32)
    phase = times[:, None] * angular[None, :]
    table = jnp.stack([jnp.cos(phase), -jnp.sin(phase)], axis=1) / math.sqrt(F)
    return table.astype(jnp.bfloat16)

def analysis_table(freq_ids):
    angular = (freq_ids + 1.0) * (math.pi / F)
    times = jnp.arange(1, STEPS + 1, dtype=jnp.float32)
    phase = angular[:, None] * times[None, :]
    return jnp.stack([jnp.cos(phase), -jnp.sin(phase)], axis=0) / math.sqrt(STEPS)

def reference(forcing_hat, mean_speed, block_order, block_flips):
    chain_ids = (jnp.arange(NBLOCKS, dtype=jnp.int32) // BPD * BPD + block_order).astype(jnp.int32)
    freq_ids = jnp.arange(F, dtype=jnp.float32)
    synth = synthesis_table(freq_ids).astype(jnp.float32)
    forcing = jnp.stack([jnp.einsum('scm,cmvrj->svrj', synth, forcing_hat[:, :, vector].astype(jnp.float32), precision=lax.Precision.HIGHEST) for vector in range(K)], axis=0)
    forcing = to_chain(forcing, chain_ids, block_flips, NBLOCKS)
    speed_chain = to_chain(mean_speed, chain_ids, block_flips, NBLOCKS)
    fields_now = jnp.zeros((K, 5, ROWS, NJ), jnp.float32)
    history = []
    for step_index in range(STEPS):
        extended = jnp.pad(fields_now, ((0, 0), (0, 0), (1, 1), (1, 1)))
        fields_now = fields_now + time_step * (tendency(extended, speed_chain) + forcing[:, step_index])
        history.append(fields_now)
    history = from_chain(jnp.stack(history, axis=1), chain_ids, block_flips, NBLOCKS)
    analysis = analysis_table(freq_ids)
    return jnp.stack([jnp.einsum('cms,svrj->cmvrj', analysis, history[vector], precision=lax.Precision.HIGHEST) for vector in range(K)], axis=2)
```

```python
import functools
import math

import jax
import jax.numpy as jnp
from jax import lax
from jax.experimental import pallas as pl
from jax.experimental.pallas import tpu as pltpu
from jax.sharding import PartitionSpec as P

F = 64
STEPS = 8
K = 2
FIELDS = 5
BLOCK_ROWS = 16
TILE = 8
TIME_STEP = 0.4
FOLD = 0.2
X_PAIR, X_CROSS, Z_PAIR = 2, 6, 1


def flipped(tile, lanes):
    return jnp.take_along_axis(tile, lanes, axis=1, mode="promise_in_bounds")


def lane_order(flag, rows):
    lane = lax.broadcasted_iota(jnp.int32, (rows, 128), 1)
    return jnp.where(flag == 1, 127 - lane, lane)


def edge_kernel(order, flips, forcing, speed, low, high):
    for out, place, start in ((low, 0, 0), (high, -1, BLOCK_ROWS - TILE)):
        block = order[place % order.shape[0]]
        lanes = lane_order(flips[block], TILE)
        rows = pl.ds(pl.multiple_of(block * BLOCK_ROWS + start, TILE), TILE)
        for k in range(K):
            for s in range(STEPS - 1):
                for v in range(FIELDS):
                    out[(k * (STEPS - 1) + s) * FIELDS + v] = flipped(forcing[k, s, v, rows, :], lanes)
        out[K * (STEPS - 1) * FIELDS] = flipped(speed[rows, :], lanes)


def step_kernel(k, order, flips, inside, forcing, speed, below, above, history, ext):
    blocks = order.shape[0]
    inner = blocks * BLOCK_ROWS
    rows = inner + 2 * TILE
    lanes = [lane_order(flips[order[p]], BLOCK_ROWS) for p in range(blocks)]
    at = [pl.ds(pl.multiple_of(order[p] * BLOCK_ROWS, BLOCK_ROWS), BLOCK_ROWS) for p in range(blocks)]
    last = K * (STEPS - 1) * FIELDS
    speed_ext = jnp.concatenate(
        [below[last]] + [flipped(speed[at[p], :], lanes[p]) for p in range(blocks)] + [above[last]], axis=0
    )
    with_up, with_down = 1.0 - speed_ext, 1.0 + speed_ext
    lane = lax.broadcasted_iota(jnp.int32, (rows, 128), 1)
    row = lax.broadcasted_iota(jnp.int32, (rows, 128), 0)
    first_lane, last_lane = lane == 0, lane == 127
    keep_low = inside[0].astype(jnp.float32)
    keep_high = inside[1].astype(jnp.float32)
    keep = jnp.where(row < TILE, keep_low, jnp.where(row >= inner + TILE, keep_high, 1.0))

    for s in range(STEPS):
        fresh = []
        for v in range(FIELDS):
            body = [flipped(forcing[k, s, v, at[p], :], lanes[p]) for p in range(blocks)]
            if s < STEPS - 1:
                unit = (k * (STEPS - 1) + s) * FIELDS + v
                lo, hi = below[unit], above[unit]
            else:
                lo = hi = jnp.zeros((TILE, 128), jnp.float32)
            fresh.append(TIME_STEP * jnp.concatenate([lo] + body + [hi], axis=0))
        if s == 0:
            state = fresh
        else:
            state = [ext[v] for v in range(FIELDS)]
            up = [pltpu.roll(a, rows - 1, 0) for a in state]
            down = [pltpu.roll(a, 1, 0) for a in state]
            right = [jnp.where(last_lane, 0.0, pltpu.roll(a, 127, 1)) for a in state]
            left = [jnp.where(first_lane, 0.0, pltpu.roll(a, 1, 1)) for a in state]
            div = (up[1] - down[1]) + (right[2] - left[2])
            extra = [div, up[3] - down[3], right[3] - left[3], div, None]
            new = []
            for v in range(FIELDS):
                total = state[v] + left[v] + right[v] + with_up * up[v] + with_down * down[v]
                if extra[v] is not None:
                    total = total - extra[v]
                new.append((FOLD * total + fresh[v]) * keep)
            state = new
        for v in range(FIELDS):
            if s < STEPS - 1:
                ext[v] = state[v]
            for p in range(blocks):
                first = TILE + p * BLOCK_ROWS
                history[s, v, at[p], :] = flipped(state[v][first : first + BLOCK_ROWS], lanes[p])


def analysis_kernel(both, low_part, history, out):
    tiles = history.shape[1]
    for pair in range(0, tiles, 2):
        x = history[:, pair : pair + 2].reshape(STEPS, 2 * TILE, 128)
        hi = x.astype(jnp.bfloat16)
        lo = (x - hi.astype(jnp.float32)).astype(jnp.bfloat16)
        hi = hi.reshape(STEPS * 2 * TILE, 128)
        lo = lo.reshape(STEPS * 2 * TILE, 128)
        y = jnp.dot(both[...], jnp.concatenate([hi, lo], axis=0), preferred_element_type=jnp.float32)
        y = y + jnp.dot(low_part[...], hi, preferred_element_type=jnp.float32)
        out[:, pair : pair + 2] = y.reshape(16, 2, TILE, 128)


def synthesis_table(freq_ids):
    angular = (freq_ids + 1.0) * (math.pi / F)
    times = jnp.arange(STEPS, dtype=jnp.float32)
    phase = times[:, None] * angular[None, :]
    table = jnp.stack([jnp.cos(phase), -jnp.sin(phase)], axis=1) / math.sqrt(F)
    return table.astype(jnp.bfloat16)


def analysis_table(freq_ids):
    angular = (freq_ids + 1.0) * (math.pi / F)
    times = jnp.arange(1, STEPS + 1, dtype=jnp.float32)
    phase = angular[:, None] * times[None, :]
    return jnp.stack([jnp.cos(phase), -jnp.sin(phase)], axis=0) / math.sqrt(STEPS)


def swap(x, mask):
    return lax.ppermute(x, "freq", [(i, i ^ mask) for i in range(lax.axis_size("freq"))])


def halves(x, bit):
    half = x.shape[1] // 2
    keep = lax.dynamic_slice_in_dim(x, bit * half, half, 1)
    send = lax.dynamic_slice_in_dim(x, (1 - bit) * half, half, 1)
    return keep, send


def joined(mine, other, bit):
    return jnp.concatenate([jnp.where(bit == 0, mine, other), jnp.where(bit == 0, other, mine)], axis=1)


def group_sum(x, order, bits):
    a, b, c = order
    keep, send = halves(x, bits[a])
    x = keep + swap(send, a)
    keep, send = halves(x, bits[b])
    x = keep + swap(send, b)
    x = x + swap(x, c)
    x = joined(x, swap(x, b), bits[b])
    return joined(x, swap(x, a), bits[a])


def smem():
    return pl.BlockSpec(memory_space=pltpu.SMEM)


def vmem():
    return pl.BlockSpec(memory_space=pltpu.VMEM)


def local(forcing_hat, mean_speed, block_order, block_flips):
    freq_local = forcing_hat.shape[1]
    rows = mean_speed.shape[0]
    freq = lax.axis_index("freq")
    x_at = freq // 2
    bits = {X_PAIR: (x_at % 2) ^ (x_at // 2), X_CROSS: x_at // 2, Z_PAIR: freq % 2}
    freq_ids = (freq * freq_local + jnp.arange(freq_local, dtype=jnp.int32)).astype(jnp.float32)
    synth = synthesis_table(freq_ids)
    forcing = jnp.einsum("scm,cmkvrj->ksvrj", synth, forcing_hat, preferred_element_type=jnp.float32)

    edge_units = K * (STEPS - 1) * FIELDS + 1
    low, high = pl.pallas_call(
        edge_kernel,
        out_shape=[jax.ShapeDtypeStruct((edge_units, TILE, 128), jnp.float32)] * 2,
        in_specs=[smem(), smem(), vmem(), vmem()],
        out_specs=[vmem(), vmem()],
        name="edges",
    )(block_order, block_flips, forcing, mean_speed)
    peers = lax.axis_size("blk")
    below = lax.ppermute(high, "blk", [(i, i + 1) for i in range(peers - 1)])
    above = lax.ppermute(low, "blk", [(i + 1, i) for i in range(peers - 1)])
    here = lax.axis_index("blk")
    inside = jnp.stack([here > 0, here < peers - 1]).astype(jnp.int32)

    table = analysis_table(freq_ids).reshape(2 * freq_local, STEPS)
    table_hi = table.astype(jnp.bfloat16)
    table_lo = (table - table_hi.astype(jnp.float32)).astype(jnp.bfloat16)
    eye = jnp.eye(2 * TILE, dtype=jnp.bfloat16)

    def spread(t):
        return (t[:, None, :, None] * eye[None, :, None, :]).reshape(2 * freq_local * 2 * TILE, STEPS * 2 * TILE)

    wide_hi, wide_lo = spread(table_hi), spread(table_lo)
    both = jnp.concatenate([wide_hi, wide_hi], axis=1)

    tiles = FIELDS * rows // TILE
    links = (X_PAIR, X_CROSS, Z_PAIR)
    sums = []
    for k in range(K):
        history = pl.pallas_call(
            functools.partial(step_kernel, k),
            out_shape=jax.ShapeDtypeStruct((STEPS, FIELDS, rows, 128), jnp.float32),
            in_specs=[smem(), smem(), smem(), vmem(), vmem(), vmem(), vmem()],
            out_specs=vmem(),
            scratch_shapes=[pltpu.VMEM((FIELDS, rows + 2 * TILE, 128), jnp.float32)],
            name=f"march{k}",
        )(block_order, block_flips, inside, forcing, mean_speed, below, above)
        history = history.reshape(STEPS, tiles, TILE, 128)
        cuts = [16, 12, 12] if k == 0 else [12, 16, 12]
        done, parts = 0, []
        for i, cut in enumerate(cuts):
            part = history[:, done : done + cut]
            parts.append(group_sum(part, [links[(i + j) % 3] for j in range(3)], bits))
            done += cut
        sums.append(jnp.concatenate(parts, axis=1))
    total = jnp.concatenate(sums, axis=1)

    group = 8
    out = pl.pallas_call(
        analysis_kernel,
        out_shape=jax.ShapeDtypeStruct((2 * freq_local, K * tiles, TILE, 128), jnp.float32),
        grid=(K * tiles // group,),
        in_specs=[
            vmem(),
            vmem(),
            pl.BlockSpec((STEPS, group, TILE, 128), lambda i: (0, i, 0, 0)),
        ],
        out_specs=pl.BlockSpec((2 * freq_local, group, TILE, 128), lambda i: (0, i, 0, 0)),
        name="analysis",
    )(both, wide_lo, total)
    return out.reshape(2, freq_local, K, FIELDS, rows, 128)


def solution(mesh):
    placed = (P(None, "freq", None, None, "blk", None), P("blk", None), P("blk"), P("blk"))
    return jax.shard_map(
        local,
        mesh=mesh,
        in_specs=placed,
        out_specs=P(None, "freq", None, None, "blk", None),
        check_vma=False,
    )
```

```python
import functools
import math

import jax
import jax.numpy as jnp
from jax import lax
from jax.experimental import pallas as pl
from jax.experimental.pallas import tpu as pltpu
from jax.sharding import PartitionSpec as P

F = 64
STEPS = 8
K = 2
FIELDS = 5
BLOCK = 16
BLOCKS = 4
LOADS = (3, 2)
TILE = 8
LANES = 128
TIME_STEP = 0.4
FOLD = 0.2
EDGES = STEPS - 1
PACKED = (EDGES + 1) // 2
UNITS_PER_K = FIELDS * PACKED
EDGE_UNITS = K * UNITS_PER_K + 1
X_PAIR, X_CROSS, Z_PAIR = 2, 6, 1
SMALL = pltpu.CompilerParams(vmem_limit_bytes=12 * 2**20)


def flipped(tile, lanes):
    return jnp.take_along_axis(tile, lanes, axis=1, mode="promise_in_bounds")


def lane_order(flag, rows):
    lane = lax.broadcasted_iota(jnp.int32, (rows, LANES), 1)
    return jnp.where(flag == 1, LANES - 1 - lane, lane)


def front_kernel(
    k, masks, order_hbm, flips_hbm, small, hat_hbm, speed_hbm, *rest
):
    low_in = high_in = None
    if k:
        low_in, high_in, _ = rest[:3]
        rest = rest[3:]
    keep, send, ends, low, high, speed, table_out, meta, token = rest[:9]
    order, flips, hat, forcing, stored_speed, sems = rest[9:]
    copies = [
        pltpu.make_async_copy(order_hbm, order, sems.at[0]),
        pltpu.make_async_copy(flips_hbm, flips, sems.at[1]),
        pltpu.make_async_copy(speed_hbm, stored_speed, sems.at[2]),
    ]
    loads, done = [], 0
    for i, fields in enumerate(LOADS):
        there = hat_hbm.at[:, k, pl.ds(done, fields)]
        loads.append(pltpu.make_async_copy(there, hat.at[:, pl.ds(done, fields)], sems.at[3 + i]))
        done += fields
    for copy in copies + loads:
        copy.start()
    token[...] = jnp.zeros_like(token)
    table = spread_synthesis(small[: 2 * TILE])
    if k:
        low[: k * UNITS_PER_K] = low_in[: k * UNITS_PER_K]
        high[: k * UNITS_PER_K] = high_in[: k * UNITS_PER_K]
        table_out[...] = spread_analysis(small[2 * TILE : 4 * TILE], small[4 * TILE :])
    for copy in copies:
        copy.wait()
    flags = [flips[order[p]] for p in range(BLOCKS)]
    lanes = [lane_order(flags[p], STEPS * BLOCK) for p in range(BLOCKS)]
    at = [pl.ds(pl.multiple_of(order[p] * BLOCK, BLOCK), BLOCK) for p in range(BLOCKS)]
    for p in range(BLOCKS):
        speed[p * BLOCK : (p + 1) * BLOCK, :] = flipped(stored_speed[at[p], :], lanes[p][:BLOCK])
    if k:
        low[EDGE_UNITS - 1] = speed[:TILE, :]
        high[EDGE_UNITS - 1] = speed[BLOCKS * BLOCK - TILE :, :]
        line = lax.broadcasted_iota(jnp.int32, (TILE, LANES), 0)
        value = jnp.zeros((TILE, LANES), jnp.int32)
        for t in range(2 * BLOCKS):
            here = line == t
            value = jnp.where(here, jnp.full((TILE, LANES), order[t // 2] * 4 + t % 2 * 2 + flags[t // 2]), value)
        meta[...] = value
    row = lax.broadcasted_iota(jnp.int32, (TILE, LANES), 0)
    done = 0
    for i, fields in enumerate(LOADS):
        loads[i].wait()
        for v in range(done, done + fields):
            for p in range(0, BLOCKS, 2):
                pair = [hat[:, v, at[p + i], :].reshape(-1, LANES) for i in range(2)]
                both = jnp.dot(table, jnp.concatenate(pair, axis=1), preferred_element_type=jnp.float32)
                for i in range(2):
                    y = flipped(both[:, i * LANES : (i + 1) * LANES], lanes[p + i]).reshape(STEPS, BLOCK, LANES)
                    forcing[:, v, (p + i) * BLOCK : (p + i + 1) * BLOCK, :] = y
                    unit = k * UNITS_PER_K + v * PACKED
                    if p + i == 0:
                        ends[:, v, :BLOCK, :] = y
                        for s in range(PACKED):
                            late = pltpu.roll(y[EDGES - 1 - s, :TILE], EDGES - s, 0)
                            low[unit + s] = jnp.where(row < EDGES - s, y[s, :TILE], late)
                    if p + i == BLOCKS - 1:
                        ends[:, v, BLOCK:, :] = y
                        for s in range(PACKED):
                            late = pltpu.roll(y[EDGES - 1 - s, TILE:], s + 1, 0)
                            high[unit + s] = jnp.where(row > s, y[s, TILE:], late)
        done += fields

    rows = BLOCKS * BLOCK
    half = rows // 2 - TILE
    upper = jnp.full((half, LANES), bit_at(masks)) == 1

    def emit(s, state):
        for v in range(FIELDS):
            first, second = state[v][TILE : TILE + half], state[v][TILE + half : TILE + 2 * half]
            keep[s, v] = jnp.where(upper, second, first)
            send[s, v] = jnp.where(upper, first, second)

    march(rows, speed[...], lambda s, v: forcing[s, v], None, emit)


def one_hot(shape, rows_are, columns_are):
    row = lax.broadcasted_iota(jnp.int32, shape, 0)
    column = lax.broadcasted_iota(jnp.int32, shape, 1)
    return (rows_are(row) == columns_are(column)).astype(jnp.float32).astype(jnp.bfloat16)


def matmul(a, b):
    return jnp.dot(a, b, preferred_element_type=jnp.float32)


def widened(small, tall, wide, unit):
    rows = one_hot((tall, small.shape[0]), lambda r: r // unit, lambda c: c)
    columns = one_hot((small.shape[1], wide), lambda r: r, lambda c: c // unit)
    whole = matmul(matmul(rows, small).astype(jnp.bfloat16), columns)
    row = lax.broadcasted_iota(jnp.int32, (tall, wide), 0)
    column = lax.broadcasted_iota(jnp.int32, (tall, wide), 1)
    return jnp.where(row % unit == column % unit, whole, 0.0).astype(jnp.bfloat16)


def spread_synthesis(small):
    return widened(small, STEPS * BLOCK, BLOCK * BLOCK, BLOCK)


def spread_analysis(high, low):
    high, low = (widened(part, BLOCK * TILE, STEPS * TILE, TILE).astype(jnp.float32) for part in (high, low))
    return jnp.concatenate([high, high, low], axis=1).astype(jnp.bfloat16)


def march(rows, speed, forcing_at, keep, emit):
    with_up, with_down = 1.0 - speed, 1.0 + speed
    lane = lax.broadcasted_iota(jnp.int32, (rows, LANES), 1)
    first_lane, last_lane = lane == 0, lane == LANES - 1
    state = None
    for s in range(STEPS):
        fresh = [TIME_STEP * forcing_at(s, v) for v in range(FIELDS)]
        if s == 0:
            state = fresh
        else:
            up = [pltpu.roll(a, rows - 1, 0) for a in state]
            down = [pltpu.roll(a, 1, 0) for a in state]
            right = [jnp.where(last_lane, 0.0, pltpu.roll(a, LANES - 1, 1)) for a in state]
            left = [jnp.where(first_lane, 0.0, pltpu.roll(a, 1, 1)) for a in state]
            div = (up[1] - down[1]) + (right[2] - left[2])
            extra = [div, up[3] - down[3], right[3] - left[3], div, None]
            new = []
            for v in range(FIELDS):
                total = state[v] + left[v] + right[v] + with_up * up[v] + with_down * down[v]
                if extra[v] is not None:
                    total = total - extra[v]
                total = FOLD * total + fresh[v]
                new.append(total if keep is None else total * keep)
            state = new
        emit(s, state)


def bit_at(masks):
    freq = lax.axis_index("freq")
    x_at = freq // 2
    bit_of = {X_PAIR: (x_at + x_at // 2) % 2, X_CROSS: x_at // 2, Z_PAIR: freq % 2}
    return jnp.where(lax.axis_index("blk") % 2 == 0, bit_of[masks[0]], bit_of[masks[1]])


def edge_kernel(masks, ends0, ends1, speed, below, above, _, keep, send, token):
    token[...] = jnp.zeros_like(token)
    inner = speed.shape[0]
    row = lax.broadcasted_iota(jnp.int32, (6 * TILE, LANES), 0)
    upper = jnp.full((TILE, LANES), bit_at(masks)) == 1
    here = lax.axis_index("blk")
    has_below = (here > 0).astype(jnp.float32)
    has_above = (here < lax.axis_size("blk") - 1).astype(jnp.float32)
    inside = jnp.where(row < TILE, has_below, jnp.where(row >= 5 * TILE, has_above, 1.0))

    def windows(lo, body, hi):
        return jnp.concatenate([lo, body, hi], axis=0)

    last = EDGE_UNITS - 1
    near_ends = jnp.concatenate([speed[: 2 * TILE, :], speed[inner - 2 * TILE :, :]], axis=0)
    speeds = windows(below[last], near_ends, above[last])
    for k, ends in enumerate((ends0, ends1)):

        def forcing_at(s, v):
            unit = k * UNITS_PER_K + v * PACKED
            if s == EDGES:
                lo = hi = jnp.zeros((TILE, LANES), jnp.float32)
            elif s < PACKED:
                lo, hi = below[unit + s], above[unit + s]
            else:
                early = EDGES - 1 - s
                lo = pltpu.roll(below[unit + early], TILE - 1 - early, 0)
                hi = pltpu.roll(above[unit + early], early + 1, 0)
            return windows(lo, ends[s, v], hi)

        def emit(s, state):
            for v in range(FIELDS):
                first, second = state[v][TILE : 2 * TILE], state[v][4 * TILE : 5 * TILE]
                keep[s, k * FIELDS + v] = jnp.where(upper, second, first)
                send[s, k * FIELDS + v] = jnp.where(upper, first, second)

        march(6 * TILE, speeds, forcing_at, inside, emit)


def bit_at(masks):
    freq = lax.axis_index("freq")
    x_at = freq // 2
    bit_of = {X_PAIR: (x_at + x_at // 2) % 2, X_CROSS: x_at // 2, Z_PAIR: freq % 2}
    return jnp.where(lax.axis_index("blk") % 2 == 0, bit_of[masks[0]], bit_of[masks[1]])


def fold_kernel(masks, mine, arrived, _, keep, send, token):
    token[...] = jnp.zeros_like(token)
    half = keep.shape[0]
    upper = jnp.full(mine.shape[2:], bit_at(masks)) == 1
    for s in range(half):
        for u in range(mine.shape[1]):
            first = mine[s, u] + arrived[s, u]
            second = mine[half + s, u] + arrived[half + s, u]
            keep[s, u] = jnp.where(upper, second, first)
            send[s, u] = jnp.where(upper, first, second)


def add_kernel(mine, arrived, _, total, token):
    token[...] = jnp.zeros_like(token)
    total[...] = mine[...] + arrived[...]


def join_kernel(masks, mine, arrived, _, whole, token):
    token[...] = jnp.zeros_like(token)
    half = mine.shape[0]
    upper = jnp.full(mine.shape[2:], bit_at(masks)) == 1
    for s in range(half):
        for u in range(mine.shape[1]):
            whole[s, u] = jnp.where(upper, arrived[s, u], mine[s, u])
            whole[half + s, u] = jnp.where(upper, mine[s, u], arrived[s, u])


def analysis_kernel(first_tile, first_unit, meta, table, history, _, *rest):
    out, token, buffer, sems = rest[-4:]
    token[...] = jnp.zeros_like(token)
    units, tiles = history.shape[1], history.shape[2] // TILE
    first = first_tile()
    copies = []
    for i in range(tiles):
        stored = meta[pl.ds(first + i, 1), 0:1][0, 0]
        tile = stored // 2
        lanes = lane_order(stored % 2, STEPS * TILE)
        for start in range(0, units, FIELDS):
            for u in range(start, start + FIELDS, 2):
                pair = []
                for j in range(u, min(u + 2, start + FIELDS)):
                    x = flipped(history[:, j, i * TILE : (i + 1) * TILE, :].reshape(STEPS * TILE, LANES), lanes)
                    hi = x.astype(jnp.bfloat16)
                    lo = (x - hi.astype(jnp.float32)).astype(jnp.bfloat16)
                    pair.append(jnp.concatenate([hi, lo, hi], axis=0))
                y = jnp.dot(table[...], jnp.concatenate(pair, axis=1), preferred_element_type=jnp.float32)
                for j in range(len(pair)):
                    part = y[:, j * LANES : (j + 1) * LANES].reshape(buffer.shape[1], TILE, LANES)
                    buffer[i, :, u + j] = part
            copy = pltpu.make_async_copy(
                buffer.at[i, :, pl.ds(start, FIELDS)],
                out.at[:, pl.ds(first_unit + start, FIELDS), tile],
                sems.at[len(copies)],
            )
            copy.start()
            copies.append(copy)
    for copy in copies:
        copy.wait()


def small_tables(freq, freq_local):
    shape = (BLOCK, LANES)
    row = lax.broadcasted_iota(jnp.int32, shape, 0)
    column = lax.broadcasted_iota(jnp.int32, shape, 1)

    def entries(cm, times, scale, valid):
        angular = ((freq * freq_local + cm % freq_local).astype(jnp.float32) + 1.0) * (math.pi / F)
        phase = times.astype(jnp.float32) * angular
        value = jnp.where(cm < freq_local, jnp.cos(phase), -jnp.sin(phase)) / math.sqrt(scale)
        return jnp.where(valid, value, 0.0)

    synthesis = entries(column, row, F, (row < STEPS) & (column < 2 * freq_local))
    analysis = entries(row, column + 1, STEPS, column < STEPS)
    high = lax.reduce_precision(analysis, 8, 7)
    return jnp.concatenate([synthesis, high, analysis - high], axis=0).astype(jnp.bfloat16)


def swap(x, masks):
    blocks, freqs = lax.axis_size("blk"), lax.axis_size("freq")
    pairs = [(b * freqs + f, b * freqs + (f ^ masks[b % 2])) for b in range(blocks) for f in range(freqs)]
    return lax.ppermute(x, ("blk", "freq"), pairs)


def vmem():
    return pl.BlockSpec(memory_space=pltpu.VMEM)


def near(x):
    return pltpu.with_memory_space_constraint(x, pltpu.VMEM)


def far(x):
    return pltpu.with_memory_space_constraint(x, pltpu.HBM)


def local(forcing_hat, mean_speed, block_order, block_flips):
    freq_local = forcing_hat.shape[1]
    rows = mean_speed.shape[0]
    freq = lax.axis_index("freq")
    cm = 2 * freq_local

    masks_of = (
        ((X_PAIR, Z_PAIR), (X_CROSS, X_PAIR), (Z_PAIR, X_CROSS)),
        ((X_PAIR, Z_PAIR), (X_CROSS, X_PAIR), (Z_PAIR, X_CROSS)),
        ((X_CROSS, X_CROSS), (Z_PAIR, Z_PAIR), (X_PAIR, X_PAIR)),
    )
    half = rows // 2 - TILE
    hbm = pl.BlockSpec(memory_space=pltpu.HBM)
    token_shape = pltpu.VMEM((TILE, LANES), jnp.float32)
    edge_shape = pltpu.VMEM((EDGE_UNITS, TILE, LANES), jnp.float32)

    def call(kernel, name, shapes, *args, token=None):
        extra = [] if token is None else [token]
        return pl.pallas_call(
            kernel,
            out_shape=list(shapes) + [token_shape],
            in_specs=[vmem()] * len(args) + [pl.BlockSpec(memory_space=pl.ANY)] * len(extra),
            out_specs=[vmem()] * (len(shapes) + 1),
            compiler_params=SMALL,
            name=name,
        )(*[near(x) for x in args], *extra)

    small = small_tables(freq, freq_local)
    hat = forcing_hat.reshape(cm, K, FIELDS, rows, LANES)
    part_shape = pltpu.VMEM((STEPS, FIELDS, half, LANES), jnp.float32)
    keep, send, ends, arrived = [None] * 3, [None] * 3, [None] * K, [None] * 3
    low = high = token = None
    for k in range(K):
        extra = [near(low), near(high), token] if k else []
        keep[k], send[k], ends[k], low, high, speed, table, meta, token = pl.pallas_call(
            functools.partial(front_kernel, k, masks_of[k][0]),
            out_shape=[
                part_shape,
                part_shape,
                pltpu.VMEM((STEPS, FIELDS, 2 * BLOCK, LANES), jnp.float32),
                edge_shape,
                edge_shape,
                pltpu.VMEM((rows, LANES), jnp.float32),
                pltpu.VMEM((BLOCK * TILE, 3 * STEPS * TILE), jnp.bfloat16),
                pltpu.VMEM((TILE, LANES), jnp.int32),
                token_shape,
            ],
            in_specs=[hbm, hbm, vmem(), hbm, hbm]
            + [vmem(), vmem(), pl.BlockSpec(memory_space=pl.ANY)][: len(extra)],
            out_specs=[vmem()] * 9,
            scratch_shapes=[
                pltpu.SMEM((BLOCKS,), jnp.int32),
                pltpu.SMEM((BLOCKS,), jnp.int32),
                pltpu.VMEM((cm, FIELDS, rows, LANES), jnp.bfloat16),
                pltpu.VMEM((STEPS, FIELDS, rows, LANES), jnp.float32),
                pltpu.VMEM((rows, LANES), jnp.float32),
                pltpu.SemaphoreType.DMA((3 + len(LOADS),)),
            ],
            compiler_params=SMALL,
            name=f"front{k}",
        )(far(block_order), far(block_flips), near(small), far(hat), far(mean_speed), *extra)
        arrived[k] = swap(send[k], masks_of[k][0])

    peers = lax.axis_size("blk")
    below = lax.ppermute(high, "blk", [(i, i + 1) for i in range(peers - 1)])
    above = lax.ppermute(low, "blk", [(i + 1, i) for i in range(peers - 1)])

    def edges():
        nonlocal token
        kernel = functools.partial(edge_kernel, masks_of[2][0])
        shape = pltpu.VMEM((STEPS, K * FIELDS, TILE, LANES), jnp.float32)
        args = (*ends, speed, below, above)
        keep[2], send[2], token = call(kernel, "edges", [shape] * 2, *args, token=token)
        arrived[2] = swap(send[2], masks_of[2][0])

    whole = [None] * 3
    other = [None] * 3

    def fold(i):
        nonlocal token
        x = keep[i]
        shape = pltpu.VMEM((x.shape[0] // 2,) + x.shape[1:], x.dtype)
        kernel = functools.partial(fold_kernel, masks_of[i][1])
        keep[i], send[i], token = call(kernel, f"fold{i}", [shape] * 2, x, arrived[i], token=token)
        arrived[i] = swap(send[i], masks_of[i][1])

    def add(i, masks):
        nonlocal token
        x = keep[i]
        keep[i], token = call(add_kernel, f"add{i}", [pltpu.VMEM(x.shape, x.dtype)], x, arrived[i], token=token)
        arrived[i] = swap(keep[i], masks)

    def join(i):
        nonlocal token
        x = keep[i]
        shape = pltpu.VMEM((x.shape[0] * 2,) + x.shape[1:], x.dtype)
        kernel = functools.partial(join_kernel, masks_of[i][1])
        whole[i], token = call(kernel, f"join{i}", [shape], x, arrived[i], token=token)
        other[i] = swap(whole[i], masks_of[i][0])

    out = None
    total_tiles = rows // TILE

    def analyse(i, x, is_other):
        nonlocal out, token
        units, tiles = x.shape[1], x.shape[2] // TILE
        extra = [] if out is None else [out]

        def first_tile():
            bit = bit_at(masks_of[i][0])
            bit = 1 - bit if is_other else bit
            return 1 + bit * (half // TILE) if i < K else bit * (total_tiles - 1)

        out, token = pl.pallas_call(
            functools.partial(analysis_kernel, first_tile, i * FIELDS if i < K else 0),
            out_shape=[
                jax.ShapeDtypeStruct((cm, K * FIELDS, total_tiles, TILE, LANES), jnp.float32),
                token_shape,
            ],
            in_specs=[vmem()] * 3 + [pl.BlockSpec(memory_space=pl.ANY)] + [hbm] * len(extra),
            out_specs=[hbm, vmem()],
            scratch_shapes=[
                pltpu.VMEM((tiles, cm, units, TILE, LANES), jnp.float32),
                pltpu.SemaphoreType.DMA((tiles * units // FIELDS,)),
            ],
            input_output_aliases={4: 0} if extra else {},
            compiler_params=SMALL,
            name=f"analysis{i}",
        )(near(meta), near(table), near(x), token, *extra)

    fold(0)
    edges()
    fold(1)
    add(0, masks_of[0][2])
    add(1, masks_of[1][2])
    fold(2)
    add(0, masks_of[0][1])
    add(1, masks_of[1][1])
    add(2, masks_of[2][2])
    join(0)
    join(1)
    add(2, masks_of[2][1])
    analyse(0, whole[0], False)
    join(2)
    analyse(1, whole[1], False)
    analyse(0, other[0], True)
    analyse(2, whole[2], False)
    analyse(1, other[1], True)
    analyse(2, other[2], True)
    return out.reshape(2, freq_local, K, FIELDS, rows, LANES)


def solution(mesh):
    placed = (P(None, "freq", None, None, "blk", None), P("blk", None), P("blk"), P("blk"))
    return jax.shard_map(
        local,
        mesh=mesh,
        in_specs=placed,
        out_specs=P(None, "freq", None, None, "blk", None),
        check_vma=False,
    )
```

```python
import functools
import math

import jax
import jax.numpy as jnp
from jax import lax
from jax.experimental import pallas as pl
from jax.experimental.pallas import tpu as pltpu
from jax.sharding import PartitionSpec as P

F = 64
STEPS = 8
K = 2
FIELDS = 5
BLOCK = 16
BLOCKS = 4
LOADS = tuple((k, start, fields) for k in range(K) for start, fields in ((0, 3), (3, 2)))
TILE = 8
LANES = 128
TIME_STEP = 0.4
FOLD = 0.2
EDGES = STEPS - 1
PACKED = (EDGES + 1) // 2
EDGE_UNITS = K * FIELDS * PACKED + 1
X_PAIR, X_CROSS, Z_PAIR = 2, 6, 1
SMALL = pltpu.CompilerParams(vmem_limit_bytes=12 * 2**20)


def flipped(tile, lanes):
    return jnp.take_along_axis(tile, lanes, axis=1, mode="promise_in_bounds")


def lane_order(flag, rows):
    lane = lax.broadcasted_iota(jnp.int32, (rows, LANES), 1)
    return jnp.where(flag == 1, LANES - 1 - lane, lane)


def synth_kernel(
    order_hbm, flips_hbm, small, hat_hbm, speed_hbm, forcing, chip_edge, far_edge, speed, table_out, meta, token, *scratch
):
    order, flips, hat, stored_speed, sems = scratch
    copies = [
        pltpu.make_async_copy(order_hbm, order, sems.at[0]),
        pltpu.make_async_copy(flips_hbm, flips, sems.at[1]),
        pltpu.make_async_copy(speed_hbm, stored_speed, sems.at[2]),
    ]
    loads = []
    for k, start, fields in LOADS:
        part = (slice(None), k, pl.ds(start, fields))
        loads.append(pltpu.make_async_copy(hat_hbm.at[part], hat.at[part], sems.at[3 + len(loads)]))
    for copy in copies + loads:
        copy.start()
    token[...] = jnp.zeros_like(token)
    table = spread_synthesis(small[: 2 * TILE])
    table_out[...] = spread_analysis(small[2 * TILE : 4 * TILE], small[4 * TILE :])
    for copy in copies:
        copy.wait()
    flags = [flips[order[p]] for p in range(BLOCKS)]
    lanes = [lane_order(flags[p], STEPS * BLOCK) for p in range(BLOCKS)]
    at = [pl.ds(pl.multiple_of(order[p] * BLOCK, BLOCK), BLOCK) for p in range(BLOCKS)]
    for p in range(BLOCKS):
        speed[p * BLOCK : (p + 1) * BLOCK, :] = flipped(stored_speed[at[p], :], lanes[p][:BLOCK])
    second = jnp.full((TILE, LANES), lax.axis_index("blk") % 2) == 1

    def put(unit, low, high):
        chip_edge[unit] = jnp.where(second, low, high)
        far_edge[unit] = jnp.where(second, high, low)

    put(EDGE_UNITS - 1, speed[:TILE, :], speed[BLOCKS * BLOCK - TILE :, :])
    line = lax.broadcasted_iota(jnp.int32, (TILE, LANES), 0)
    value = jnp.zeros((TILE, LANES), jnp.int32)
    for t in range(2 * BLOCKS):
        value = jnp.where(line == t, jnp.full((TILE, LANES), order[t // 2] * 4 + t % 2 * 2 + flags[t // 2]), value)
    meta[...] = value
    for load, (k, start, fields) in zip(loads, LOADS):
        load.wait()
        for v in range(start, start + fields):
            lows, highs = [], []
            for p in range(0, BLOCKS, 2):
                pair = [hat[:, k, v, at[p + i], :].reshape(-1, LANES) for i in range(2)]
                both = matmul(table, jnp.concatenate(pair, axis=1))
                for i in range(2):
                    y = flipped(both[:, i * LANES : (i + 1) * LANES], lanes[p + i]).reshape(STEPS, BLOCK, LANES)
                    forcing[k, :, v, (p + i) * BLOCK : (p + i + 1) * BLOCK, :] = y
                    if p + i == 0:
                        for s in range(PACKED):
                            late = pltpu.roll(y[EDGES - 1 - s, :TILE], EDGES - s, 0)
                            lows.append(jnp.where(line < EDGES - s, y[s, :TILE], late))
                    if p + i == BLOCKS - 1:
                        for s in range(PACKED):
                            late = pltpu.roll(y[EDGES - 1 - s, TILE:], s + 1, 0)
                            highs.append(jnp.where(line > s, y[s, TILE:], late))
            for s in range(PACKED):
                put((k * FIELDS + v) * PACKED + s, lows[s], highs[s])


def inner_kernel(k, masks, forcing, speed, _, keep, send, token):
    token[...] = jnp.zeros_like(token)
    rows = speed.shape[0]
    half = rows // 2 - TILE
    upper = jnp.full((half, LANES), bit_at(masks)) == 1

    def emit(s, state):
        for v in range(FIELDS):
            first, second = state[v][TILE : TILE + half], state[v][TILE + half : TILE + 2 * half]
            keep[s, v] = jnp.where(upper, second, first)
            send[s, v] = jnp.where(upper, first, second)

    march(rows, speed[...], lambda s, v: forcing[k, s, v], None, emit)


def one_hot(shape, rows_are, columns_are):
    row = lax.broadcasted_iota(jnp.int32, shape, 0)
    column = lax.broadcasted_iota(jnp.int32, shape, 1)
    return (rows_are(row) == columns_are(column)).astype(jnp.float32).astype(jnp.bfloat16)


def matmul(a, b):
    return jnp.dot(a, b, preferred_element_type=jnp.float32)


def widened(small, tall, wide, unit):
    rows = one_hot((tall, small.shape[0]), lambda r: r // unit, lambda c: c)
    columns = one_hot((small.shape[1], wide), lambda r: r, lambda c: c // unit)
    whole = matmul(matmul(rows, small).astype(jnp.bfloat16), columns)
    row = lax.broadcasted_iota(jnp.int32, (tall, wide), 0)
    column = lax.broadcasted_iota(jnp.int32, (tall, wide), 1)
    return jnp.where(row % unit == column % unit, whole, 0.0).astype(jnp.bfloat16)


def spread_synthesis(small):
    return widened(small, STEPS * BLOCK, BLOCK * BLOCK, BLOCK)


def spread_analysis(high, low):
    high, low = (widened(part, BLOCK * TILE, STEPS * TILE, TILE).astype(jnp.float32) for part in (high, low))
    return jnp.concatenate([high, high, low], axis=1).astype(jnp.bfloat16)


def march(rows, speed, forcing_at, keep, emit):
    with_up, with_down = 1.0 - speed, 1.0 + speed
    lane = lax.broadcasted_iota(jnp.int32, (rows, LANES), 1)
    first_lane, last_lane = lane == 0, lane == LANES - 1
    state = None
    for s in range(STEPS):
        fresh = [TIME_STEP * forcing_at(s, v) for v in range(FIELDS)]
        if s == 0:
            state = fresh
        else:
            up = [pltpu.roll(a, rows - 1, 0) for a in state]
            down = [pltpu.roll(a, 1, 0) for a in state]
            right = [jnp.where(last_lane, 0.0, pltpu.roll(a, LANES - 1, 1)) for a in state]
            left = [jnp.where(first_lane, 0.0, pltpu.roll(a, 1, 1)) for a in state]
            div = (up[1] - down[1]) + (right[2] - left[2])
            extra = [div, up[3] - down[3], right[3] - left[3], div, None]
            new = []
            for v in range(FIELDS):
                total = state[v] + left[v] + right[v] + with_up * up[v] + with_down * down[v]
                if extra[v] is not None:
                    total = total - extra[v]
                total = FOLD * total + fresh[v]
                new.append(total if keep is None else total * keep)
            state = new
        emit(s, state)


def bit_at(masks):
    freq = lax.axis_index("freq")
    x_at = freq // 2
    bit_of = {X_PAIR: (x_at + x_at // 2) % 2, X_CROSS: x_at // 2, Z_PAIR: freq % 2}
    return jnp.where(lax.axis_index("blk") % 2 == 0, bit_of[masks[0]], bit_of[masks[1]])


def edge_kernel(masks, forcing, speed, from_chip, from_far, _, keep, send, token):
    token[...] = jnp.zeros_like(token)
    inner = speed.shape[0]
    row = lax.broadcasted_iota(jnp.int32, (6 * TILE, LANES), 0)
    upper = jnp.full((TILE, LANES), bit_at(masks)) == 1
    here = lax.axis_index("blk")
    has_below = (here > 0).astype(jnp.float32)
    has_above = (here < lax.axis_size("blk") - 1).astype(jnp.float32)
    inside = jnp.where(row < TILE, has_below, jnp.where(row >= 5 * TILE, has_above, 1.0))

    second = jnp.full((TILE, LANES), here % 2) == 1

    def halos(unit):
        chip, far = from_chip[unit], from_far[unit]
        return jnp.where(second, chip, far), jnp.where(second, far, chip)

    def windows(lo, body, hi):
        return jnp.concatenate([lo, body, hi], axis=0)

    below, above = halos(EDGE_UNITS - 1)
    near_ends = jnp.concatenate([speed[: 2 * TILE, :], speed[inner - 2 * TILE :, :]], axis=0)
    speeds = windows(below, near_ends, above)
    for k in range(K):

        def forcing_at(s, v):
            unit = (k * FIELDS + v) * PACKED
            if s == EDGES:
                lo = hi = jnp.zeros((TILE, LANES), jnp.float32)
            elif s < PACKED:
                lo, hi = halos(unit + s)
            else:
                early = EDGES - 1 - s
                lo, hi = halos(unit + early)
                lo = pltpu.roll(lo, TILE - 1 - early, 0)
                hi = pltpu.roll(hi, early + 1, 0)
            ends = [forcing[k, s, v, : 2 * TILE], forcing[k, s, v, inner - 2 * TILE :]]
            return windows(lo, jnp.concatenate(ends, axis=0), hi)

        def emit(s, state):
            for v in range(FIELDS):
                first, second = state[v][TILE : 2 * TILE], state[v][4 * TILE : 5 * TILE]
                keep[s, k * FIELDS + v] = jnp.where(upper, second, first)
                send[s, k * FIELDS + v] = jnp.where(upper, first, second)

        march(6 * TILE, speeds, forcing_at, inside, emit)


def bit_at(masks):
    freq = lax.axis_index("freq")
    x_at = freq // 2
    bit_of = {X_PAIR: (x_at + x_at // 2) % 2, X_CROSS: x_at // 2, Z_PAIR: freq % 2}
    return jnp.where(lax.axis_index("blk") % 2 == 0, bit_of[masks[0]], bit_of[masks[1]])


def fold_kernel(masks, mine, arrived, _, keep, send, token):
    token[...] = jnp.zeros_like(token)
    half = keep.shape[0]
    upper = jnp.full(mine.shape[2:], bit_at(masks)) == 1
    for s in range(half):
        for u in range(mine.shape[1]):
            first = mine[s, u] + arrived[s, u]
            second = mine[half + s, u] + arrived[half + s, u]
            keep[s, u] = jnp.where(upper, second, first)
            send[s, u] = jnp.where(upper, first, second)


def add_kernel(mine, arrived, _, total, token):
    token[...] = jnp.zeros_like(token)
    total[...] = mine[...] + arrived[...]


def join_kernel(masks, mine, arrived, _, whole, token):
    token[...] = jnp.zeros_like(token)
    half = mine.shape[0]
    upper = jnp.full(mine.shape[2:], bit_at(masks)) == 1
    for s in range(half):
        for u in range(mine.shape[1]):
            whole[s, u] = jnp.where(upper, arrived[s, u], mine[s, u])
            whole[half + s, u] = jnp.where(upper, mine[s, u], arrived[s, u])


def analysis_kernel(first_tile, first_unit, meta, table, history, _, *rest):
    out, token, buffer, sems = rest[-4:]
    token[...] = jnp.zeros_like(token)
    units, tiles = history.shape[1], history.shape[2] // TILE
    first = first_tile()
    copies = []
    for i in range(tiles):
        stored = meta[pl.ds(first + i, 1), 0:1][0, 0]
        tile = stored // 2
        lanes = lane_order(stored % 2, STEPS * TILE)
        for start in range(0, units, FIELDS):
            for u in range(start, start + FIELDS, 2):
                pair = []
                for j in range(u, min(u + 2, start + FIELDS)):
                    x = flipped(history[:, j, i * TILE : (i + 1) * TILE, :].reshape(STEPS * TILE, LANES), lanes)
                    hi = x.astype(jnp.bfloat16)
                    lo = (x - hi.astype(jnp.float32)).astype(jnp.bfloat16)
                    pair.append(jnp.concatenate([hi, lo, hi], axis=0))
                y = jnp.dot(table[...], jnp.concatenate(pair, axis=1), preferred_element_type=jnp.float32)
                for j in range(len(pair)):
                    part = y[:, j * LANES : (j + 1) * LANES].reshape(buffer.shape[1], TILE, LANES)
                    buffer[i, :, u + j] = part
            copy = pltpu.make_async_copy(
                buffer.at[i, :, pl.ds(start, FIELDS)],
                out.at[:, pl.ds(first_unit + start, FIELDS), tile],
                sems.at[len(copies)],
            )
            copy.start()
            copies.append(copy)
    for copy in copies:
        copy.wait()


def small_tables(freq, freq_local):
    shape = (BLOCK, LANES)
    row = lax.broadcasted_iota(jnp.int32, shape, 0)
    column = lax.broadcasted_iota(jnp.int32, shape, 1)

    def entries(cm, times, scale, valid):
        angular = ((freq * freq_local + cm % freq_local).astype(jnp.float32) + 1.0) * (math.pi / F)
        phase = times.astype(jnp.float32) * angular
        value = jnp.where(cm < freq_local, jnp.cos(phase), -jnp.sin(phase)) / math.sqrt(scale)
        return jnp.where(valid, value, 0.0)

    synthesis = entries(column, row, F, (row < STEPS) & (column < 2 * freq_local))
    analysis = entries(row, column + 1, STEPS, column < STEPS)
    high = lax.reduce_precision(analysis, 8, 7)
    return jnp.concatenate([synthesis, high, analysis - high], axis=0).astype(jnp.bfloat16)


def swap(x, masks):
    blocks, freqs = lax.axis_size("blk"), lax.axis_size("freq")
    pairs = [(b * freqs + f, b * freqs + (f ^ masks[b % 2])) for b in range(blocks) for f in range(freqs)]
    return lax.ppermute(x, ("blk", "freq"), pairs)


def vmem():
    return pl.BlockSpec(memory_space=pltpu.VMEM)


def near(x):
    return pltpu.with_memory_space_constraint(x, pltpu.VMEM)


def far(x):
    return pltpu.with_memory_space_constraint(x, pltpu.HBM)


def local(forcing_hat, mean_speed, block_order, block_flips):
    freq_local = forcing_hat.shape[1]
    rows = mean_speed.shape[0]
    freq = lax.axis_index("freq")
    cm = 2 * freq_local

    inner_masks = ((X_PAIR, X_CROSS), (Z_PAIR, Z_PAIR), (X_CROSS, X_PAIR))
    edge_masks = ((X_PAIR, X_CROSS), (Z_PAIR, Z_PAIR), (X_CROSS, X_PAIR))
    masks_of = (inner_masks, inner_masks, edge_masks)
    half = rows // 2 - TILE
    hbm = pl.BlockSpec(memory_space=pltpu.HBM)
    token_shape = pltpu.VMEM((TILE, LANES), jnp.float32)

    def call(kernel, name, shapes, *args, token=None):
        extra = [] if token is None else [token]
        return pl.pallas_call(
            kernel,
            out_shape=list(shapes) + [token_shape],
            in_specs=[vmem()] * len(args) + [pl.BlockSpec(memory_space=pl.ANY)] * len(extra),
            out_specs=[vmem()] * (len(shapes) + 1),
            compiler_params=SMALL,
            name=name,
        )(*[near(x) for x in args], *extra)

    small = small_tables(freq, freq_local)
    hat = forcing_hat.reshape(cm, K, FIELDS, rows, LANES)
    edge_shape = pltpu.VMEM((EDGE_UNITS, TILE, LANES), jnp.float32)
    forcing, chip_edge, far_edge, speed, table, meta, token = pl.pallas_call(
        synth_kernel,
        out_shape=[
            pltpu.VMEM((K, STEPS, FIELDS, rows, LANES), jnp.float32),
            edge_shape,
            edge_shape,
            pltpu.VMEM((rows, LANES), jnp.float32),
            pltpu.VMEM((BLOCK * TILE, 3 * STEPS * TILE), jnp.bfloat16),
            pltpu.VMEM((TILE, LANES), jnp.int32),
            token_shape,
        ],
        in_specs=[hbm, hbm, vmem(), hbm, hbm],
        out_specs=[vmem()] * 7,
        scratch_shapes=[
            pltpu.SMEM((BLOCKS,), jnp.int32),
            pltpu.SMEM((BLOCKS,), jnp.int32),
            pltpu.VMEM((cm, K, FIELDS, rows, LANES), jnp.bfloat16),
            pltpu.VMEM((rows, LANES), jnp.float32),
            pltpu.SemaphoreType.DMA((3 + len(LOADS),)),
        ],
        compiler_params=SMALL,
        name="synthesis",
    )(far(block_order), far(block_flips), near(small), far(hat), far(mean_speed))

    peers = lax.axis_size("blk")
    from_chip = lax.ppermute(chip_edge, "blk", [(i, i ^ 1) for i in range(peers)])
    joints = [(i, i + 1) for i in range(1, peers - 1, 2)]
    from_far = lax.ppermute(far_edge, "blk", joints + [(j, i) for i, j in joints])

    keep, send, arrived = [None] * 3, [None] * 3, [None] * 3
    for k in range(K):
        kernel = functools.partial(inner_kernel, k, masks_of[k][0])
        shape = pltpu.VMEM((STEPS, FIELDS, half, LANES), jnp.float32)
        keep[k], send[k], token = call(kernel, f"inner{k}", [shape] * 2, forcing, speed, token=token)
        arrived[k] = swap(send[k], masks_of[k][0])

    def edges():
        nonlocal token
        kernel = functools.partial(edge_kernel, masks_of[2][0])
        shape = pltpu.VMEM((STEPS, K * FIELDS, TILE, LANES), jnp.float32)
        args = (forcing, speed, from_chip, from_far)
        keep[2], send[2], token = call(kernel, "edges", [shape] * 2, *args, token=token)
        arrived[2] = swap(send[2], masks_of[2][0])

    whole = [None] * 3
    other = [None] * 3

    def fold(i):
        nonlocal token
        x = keep[i]
        shape = pltpu.VMEM((x.shape[0] // 2,) + x.shape[1:], x.dtype)
        kernel = functools.partial(fold_kernel, masks_of[i][1])
        keep[i], send[i], token = call(kernel, f"fold{i}", [shape] * 2, x, arrived[i], token=token)
        arrived[i] = swap(send[i], masks_of[i][1])

    def add(i, masks):
        nonlocal token
        x = keep[i]
        keep[i], token = call(add_kernel, f"add{i}", [pltpu.VMEM(x.shape, x.dtype)], x, arrived[i], token=token)
        arrived[i] = swap(keep[i], masks)

    def join(i):
        nonlocal token
        x = keep[i]
        shape = pltpu.VMEM((x.shape[0] * 2,) + x.shape[1:], x.dtype)
        kernel = functools.partial(join_kernel, masks_of[i][1])
        whole[i], token = call(kernel, f"join{i}", [shape], x, arrived[i], token=token)
        other[i] = swap(whole[i], masks_of[i][0])

    out = None
    total_tiles = rows // TILE

    def analyse(i, x, is_other):
        nonlocal out, token
        units, tiles = x.shape[1], x.shape[2] // TILE
        extra = [] if out is None else [out]

        def first_tile():
            bit = bit_at(masks_of[i][0])
            bit = 1 - bit if is_other else bit
            return 1 + bit * (half // TILE) if i < K else bit * (total_tiles - 1)

        out, token = pl.pallas_call(
            functools.partial(analysis_kernel, first_tile, i * FIELDS if i < K else 0),
            out_shape=[
                jax.ShapeDtypeStruct((cm, K * FIELDS, total_tiles, TILE, LANES), jnp.float32),
                token_shape,
            ],
            in_specs=[vmem()] * 3 + [pl.BlockSpec(memory_space=pl.ANY)] + [hbm] * len(extra),
            out_specs=[hbm, vmem()],
            scratch_shapes=[
                pltpu.VMEM((tiles, cm, units, TILE, LANES), jnp.float32),
                pltpu.SemaphoreType.DMA((tiles * units // FIELDS,)),
            ],
            input_output_aliases={4: 0} if extra else {},
            compiler_params=SMALL,
            name=f"analysis{i}",
        )(near(meta), near(table), near(x), token, *extra)

    fold(0)
    edges()
    fold(1)
    add(0, masks_of[0][2])
    add(1, masks_of[1][2])
    fold(2)
    add(0, masks_of[0][1])
    add(1, masks_of[1][1])
    add(2, masks_of[2][2])
    join(0)
    join(1)
    add(2, masks_of[2][1])
    analyse(0, whole[0], False)
    analyse(1, whole[1], False)
    join(2)
    analyse(0, other[0], True)
    analyse(2, whole[2], False)
    analyse(1, other[1], True)
    analyse(2, other[2], True)
    return out.reshape(2, freq_local, K, FIELDS, rows, LANES)


def solution(mesh):
    placed = (P(None, "freq", None, None, "blk", None), P("blk", None), P("blk"), P("blk"))
    return jax.shard_map(
        local,
        mesh=mesh,
        in_specs=placed,
        out_specs=P(None, "freq", None, None, "blk", None),
        check_vma=False,
    )
```

```python
import functools
import math

import jax
import jax.numpy as jnp
from jax import lax
from jax.experimental import pallas as pl
from jax.experimental.pallas import tpu as pltpu
from jax.sharding import PartitionSpec as P

F = 64
STEPS = 8
K = 2
FIELDS = 5
BLOCK = 16
BLOCKS = 4
LOADS = tuple((k, start, fields) for k in range(K) for start, fields in ((0, 3), (3, 2)))
TILE = 8
LANES = 128
TIME_STEP = 0.4
FOLD = 0.2
EDGES = STEPS - 1
PACKED = (EDGES + 1) // 2
EDGE_UNITS = K * FIELDS * PACKED + 1
X_PAIR, X_CROSS, Z_PAIR = 2, 6, 1
SMALL = pltpu.CompilerParams(vmem_limit_bytes=12 * 2**20)


def flipped(tile, lanes):
    return jnp.take_along_axis(tile, lanes, axis=1, mode="promise_in_bounds")


def lane_order(flag, rows):
    lane = lax.broadcasted_iota(jnp.int32, (rows, LANES), 1)
    return jnp.where(flag == 1, LANES - 1 - lane, lane)


def synth_kernel(
    order_hbm, flips_hbm, small, hat_hbm, speed_hbm, forcing, chip_edge, far_edge, speed, table_out, meta, token, *scratch
):
    order, flips, hat, stored_speed, sems = scratch
    copies = [
        pltpu.make_async_copy(order_hbm, order, sems.at[0]),
        pltpu.make_async_copy(flips_hbm, flips, sems.at[1]),
        pltpu.make_async_copy(speed_hbm, stored_speed, sems.at[2]),
    ]
    loads = []
    for k, start, fields in LOADS:
        part = (slice(None), k, pl.ds(start, fields))
        loads.append(pltpu.make_async_copy(hat_hbm.at[part], hat.at[part], sems.at[3 + len(loads)]))
    for copy in copies + loads:
        copy.start()
    token[...] = jnp.zeros_like(token)
    table = spread_synthesis(small[: 2 * TILE])
    table_out[...] = spread_analysis(small[2 * TILE : 4 * TILE], small[4 * TILE :])
    for copy in copies:
        copy.wait()
    flags = [flips[order[p]] for p in range(BLOCKS)]
    lanes = [lane_order(flags[p], STEPS * BLOCK) for p in range(BLOCKS)]
    at = [pl.ds(pl.multiple_of(order[p] * BLOCK, BLOCK), BLOCK) for p in range(BLOCKS)]
    for p in range(BLOCKS):
        speed[p * BLOCK : (p + 1) * BLOCK, :] = flipped(stored_speed[at[p], :], lanes[p][:BLOCK])
    second = jnp.full((TILE, LANES), lax.axis_index("blk") % 2) == 1

    def put(unit, low, high):
        chip_edge[unit] = jnp.where(second, low, high)
        far_edge[unit] = jnp.where(second, high, low)

    put(EDGE_UNITS - 1, speed[:TILE, :], speed[BLOCKS * BLOCK - TILE :, :])
    line = lax.broadcasted_iota(jnp.int32, (TILE, LANES), 0)
    value = jnp.zeros((TILE, LANES), jnp.int32)
    for t in range(2 * BLOCKS):
        value = jnp.where(line == t, jnp.full((TILE, LANES), order[t // 2] * 4 + t % 2 * 2 + flags[t // 2]), value)
    meta[...] = value
    for load, (k, start, fields) in zip(loads, LOADS):
        load.wait()
        for v in range(start, start + fields):
            lows, highs = [], []
            for p in range(0, BLOCKS, 2):
                pair = [hat[:, k, v, at[p + i], :].reshape(-1, LANES) for i in range(2)]
                both = matmul(table, jnp.concatenate(pair, axis=1))
                for i in range(2):
                    y = flipped(both[:, i * LANES : (i + 1) * LANES], lanes[p + i]).reshape(STEPS, BLOCK, LANES)
                    forcing[k, :, v, (p + i) * BLOCK : (p + i + 1) * BLOCK, :] = y
                    if p + i == 0:
                        for s in range(PACKED):
                            late = pltpu.roll(y[EDGES - 1 - s, :TILE], EDGES - s, 0)
                            lows.append(jnp.where(line < EDGES - s, y[s, :TILE], late))
                    if p + i == BLOCKS - 1:
                        for s in range(PACKED):
                            late = pltpu.roll(y[EDGES - 1 - s, TILE:], s + 1, 0)
                            highs.append(jnp.where(line > s, y[s, TILE:], late))
            for s in range(PACKED):
                put((k * FIELDS + v) * PACKED + s, lows[s], highs[s])


def inner_kernel(k, masks, forcing, speed, _, keep, send, token):
    token[...] = jnp.zeros_like(token)
    rows = speed.shape[0]
    half = rows // 2 - TILE
    upper = jnp.full((half, LANES), bit_at(masks)) == 1

    def emit(s, state):
        for v in range(FIELDS):
            first, second = state[v][TILE : TILE + half], state[v][TILE + half : TILE + 2 * half]
            keep[s, v] = jnp.where(upper, second, first)
            send[s, v] = jnp.where(upper, first, second)

    march(rows, speed[...], lambda s, v: forcing[k, s, v], None, emit)


def one_hot(shape, rows_are, columns_are):
    row = lax.broadcasted_iota(jnp.int32, shape, 0)
    column = lax.broadcasted_iota(jnp.int32, shape, 1)
    return (rows_are(row) == columns_are(column)).astype(jnp.float32).astype(jnp.bfloat16)


def matmul(a, b):
    return jnp.dot(a, b, preferred_element_type=jnp.float32)


def widened(small, tall, wide, unit):
    rows = one_hot((tall, small.shape[0]), lambda r: r // unit, lambda c: c)
    columns = one_hot((small.shape[1], wide), lambda r: r, lambda c: c // unit)
    whole = matmul(matmul(rows, small).astype(jnp.bfloat16), columns)
    row = lax.broadcasted_iota(jnp.int32, (tall, wide), 0)
    column = lax.broadcasted_iota(jnp.int32, (tall, wide), 1)
    return jnp.where(row % unit == column % unit, whole, 0.0).astype(jnp.bfloat16)


def spread_synthesis(small):
    return widened(small, STEPS * BLOCK, BLOCK * BLOCK, BLOCK)


def spread_analysis(high, low):
    high, low = (widened(part, BLOCK * TILE, STEPS * TILE, TILE).astype(jnp.float32) for part in (high, low))
    return jnp.concatenate([high, high, low], axis=1).astype(jnp.bfloat16)


def march(rows, speed, forcing_at, keep, emit):
    with_up, with_down = 1.0 - speed, 1.0 + speed
    lane = lax.broadcasted_iota(jnp.int32, (rows, LANES), 1)
    first_lane, last_lane = lane == 0, lane == LANES - 1
    state = None
    for s in range(STEPS):
        fresh = [TIME_STEP * forcing_at(s, v) for v in range(FIELDS)]
        if s == 0:
            state = fresh
        else:
            up = [pltpu.roll(a, rows - 1, 0) for a in state]
            down = [pltpu.roll(a, 1, 0) for a in state]
            right = [jnp.where(last_lane, 0.0, pltpu.roll(a, LANES - 1, 1)) for a in state]
            left = [jnp.where(first_lane, 0.0, pltpu.roll(a, 1, 1)) for a in state]
            div = (up[1] - down[1]) + (right[2] - left[2])
            extra = [div, up[3] - down[3], right[3] - left[3], div, None]
            new = []
            for v in range(FIELDS):
                total = state[v] + left[v] + right[v] + with_up * up[v] + with_down * down[v]
                if extra[v] is not None:
                    total = total - extra[v]
                total = FOLD * total + fresh[v]
                new.append(total if keep is None else total * keep)
            state = new
        emit(s, state)


def bit_at(masks):
    freq = lax.axis_index("freq")
    x_at = freq // 2
    bit_of = {X_PAIR: (x_at + x_at // 2) % 2, X_CROSS: x_at // 2, Z_PAIR: freq % 2}
    return jnp.where(lax.axis_index("blk") % 2 == 0, bit_of[masks[0]], bit_of[masks[1]])


def edge_kernel(masks, forcing, speed, from_chip, from_far, _, keep, send, token):
    token[...] = jnp.zeros_like(token)
    inner = speed.shape[0]
    row = lax.broadcasted_iota(jnp.int32, (6 * TILE, LANES), 0)
    upper = jnp.full((TILE, LANES), bit_at(masks)) == 1
    here = lax.axis_index("blk")
    has_below = (here > 0).astype(jnp.float32)
    has_above = (here < lax.axis_size("blk") - 1).astype(jnp.float32)
    inside = jnp.where(row < TILE, has_below, jnp.where(row >= 5 * TILE, has_above, 1.0))

    second = jnp.full((TILE, LANES), here % 2) == 1

    def halos(unit):
        chip, far = from_chip[unit], from_far[unit]
        return jnp.where(second, chip, far), jnp.where(second, far, chip)

    def windows(lo, body, hi):
        return jnp.concatenate([lo, body, hi], axis=0)

    below, above = halos(EDGE_UNITS - 1)
    near_ends = jnp.concatenate([speed[: 2 * TILE, :], speed[inner - 2 * TILE :, :]], axis=0)
    speeds = windows(below, near_ends, above)
    for k in range(K):

        def forcing_at(s, v):
            unit = (k * FIELDS + v) * PACKED
            if s == EDGES:
                lo = hi = jnp.zeros((TILE, LANES), jnp.float32)
            elif s < PACKED:
                lo, hi = halos(unit + s)
            else:
                early = EDGES - 1 - s
                lo, hi = halos(unit + early)
                lo = pltpu.roll(lo, TILE - 1 - early, 0)
                hi = pltpu.roll(hi, early + 1, 0)
            ends = [forcing[k, s, v, : 2 * TILE], forcing[k, s, v, inner - 2 * TILE :]]
            return windows(lo, jnp.concatenate(ends, axis=0), hi)

        def emit(s, state):
            for v in range(FIELDS):
                first, second = state[v][TILE : 2 * TILE], state[v][4 * TILE : 5 * TILE]
                keep[s, k * FIELDS + v] = jnp.where(upper, second, first)
                send[s, k * FIELDS + v] = jnp.where(upper, first, second)

        march(6 * TILE, speeds, forcing_at, inside, emit)


def bit_at(masks):
    freq = lax.axis_index("freq")
    x_at = freq // 2
    bit_of = {X_PAIR: (x_at + x_at // 2) % 2, X_CROSS: x_at // 2, Z_PAIR: freq % 2}
    return jnp.where(lax.axis_index("blk") % 2 == 0, bit_of[masks[0]], bit_of[masks[1]])


def fold_kernel(masks, mine, arrived, _, keep, send, token):
    token[...] = jnp.zeros_like(token)
    half = keep.shape[0]
    upper = jnp.full(mine.shape[2:], bit_at(masks)) == 1
    for s in range(half):
        for u in range(mine.shape[1]):
            first = mine[s, u] + arrived[s, u]
            second = mine[half + s, u] + arrived[half + s, u]
            keep[s, u] = jnp.where(upper, second, first)
            send[s, u] = jnp.where(upper, first, second)


def add_kernel(mine, arrived, _, total, token):
    token[...] = jnp.zeros_like(token)
    total[...] = mine[...] + arrived[...]


def join_kernel(masks, mine, arrived, _, whole, token):
    token[...] = jnp.zeros_like(token)
    half = mine.shape[0]
    upper = jnp.full(mine.shape[2:], bit_at(masks)) == 1
    for s in range(half):
        for u in range(mine.shape[1]):
            whole[s, u] = jnp.where(upper, arrived[s, u], mine[s, u])
            whole[half + s, u] = jnp.where(upper, mine[s, u], arrived[s, u])


def analysis_kernel(first_tile, first_unit, meta, table, history, _, *rest):
    out, token, buffer, sems = rest[-4:]
    token[...] = jnp.zeros_like(token)
    units, tiles = history.shape[1], history.shape[2] // TILE
    first = first_tile()
    copies = []
    for i in range(tiles):
        stored = meta[pl.ds(first + i, 1), 0:1][0, 0]
        tile = stored // 2
        lanes = lane_order(stored % 2, STEPS * TILE)
        for start in range(0, units, FIELDS):
            for u in range(start, start + FIELDS, 2):
                pair = []
                for j in range(u, min(u + 2, start + FIELDS)):
                    x = flipped(history[:, j, i * TILE : (i + 1) * TILE, :].reshape(STEPS * TILE, LANES), lanes)
                    hi = x.astype(jnp.bfloat16)
                    lo = (x - hi.astype(jnp.float32)).astype(jnp.bfloat16)
                    pair.append(jnp.concatenate([hi, lo, hi], axis=0))
                y = jnp.dot(table[...], jnp.concatenate(pair, axis=1), preferred_element_type=jnp.float32)
                for j in range(len(pair)):
                    part = y[:, j * LANES : (j + 1) * LANES].reshape(buffer.shape[1], TILE, LANES)
                    buffer[i, :, u + j] = part
            copy = pltpu.make_async_copy(
                buffer.at[i, :, pl.ds(start, FIELDS)],
                out.at[:, pl.ds(first_unit + start, FIELDS), tile],
                sems.at[len(copies)],
            )
            copies.append(copy)
    for copy in copies:
        copy.start()
    for copy in copies:
        copy.wait()


def small_tables(freq, freq_local):
    shape = (BLOCK, LANES)
    row = lax.broadcasted_iota(jnp.int32, shape, 0)
    column = lax.broadcasted_iota(jnp.int32, shape, 1)

    def entries(cm, times, scale, valid):
        angular = ((freq * freq_local + cm % freq_local).astype(jnp.float32) + 1.0) * (math.pi / F)
        phase = times.astype(jnp.float32) * angular
        value = jnp.where(cm < freq_local, jnp.cos(phase), -jnp.sin(phase)) / math.sqrt(scale)
        return jnp.where(valid, value, 0.0)

    synthesis = entries(column, row, F, (row < STEPS) & (column < 2 * freq_local))
    analysis = entries(row, column + 1, STEPS, column < STEPS)
    high = lax.reduce_precision(analysis, 8, 7)
    return jnp.concatenate([synthesis, high, analysis - high], axis=0).astype(jnp.bfloat16)


def swap(x, masks):
    blocks, freqs = lax.axis_size("blk"), lax.axis_size("freq")
    pairs = [(b * freqs + f, b * freqs + (f ^ masks[b % 2])) for b in range(blocks) for f in range(freqs)]
    return lax.ppermute(x, ("blk", "freq"), pairs)


def vmem():
    return pl.BlockSpec(memory_space=pltpu.VMEM)


def near(x):
    return pltpu.with_memory_space_constraint(x, pltpu.VMEM)


def far(x):
    return pltpu.with_memory_space_constraint(x, pltpu.HBM)


def local(forcing_hat, mean_speed, block_order, block_flips):
    freq_local = forcing_hat.shape[1]
    rows = mean_speed.shape[0]
    freq = lax.axis_index("freq")
    cm = 2 * freq_local

    inner_masks = ((X_PAIR, X_CROSS), (Z_PAIR, Z_PAIR), (X_CROSS, X_PAIR))
    edge_masks = ((X_PAIR, X_CROSS), (Z_PAIR, Z_PAIR), (X_CROSS, X_PAIR))
    masks_of = (inner_masks, inner_masks, edge_masks)
    half = rows // 2 - TILE
    hbm = pl.BlockSpec(memory_space=pltpu.HBM)
    token_shape = pltpu.VMEM((TILE, LANES), jnp.float32)

    def call(kernel, name, shapes, *args, token=None):
        extra = [] if token is None else [token]
        return pl.pallas_call(
            kernel,
            out_shape=list(shapes) + [token_shape],
            in_specs=[vmem()] * len(args) + [pl.BlockSpec(memory_space=pl.ANY)] * len(extra),
            out_specs=[vmem()] * (len(shapes) + 1),
            compiler_params=SMALL,
            name=name,
        )(*[near(x) for x in args], *extra)

    small = small_tables(freq, freq_local)
    hat = forcing_hat.reshape(cm, K, FIELDS, rows, LANES)
    edge_shape = pltpu.VMEM((EDGE_UNITS, TILE, LANES), jnp.float32)
    forcing, chip_edge, far_edge, speed, table, meta, token = pl.pallas_call(
        synth_kernel,
        out_shape=[
            pltpu.VMEM((K, STEPS, FIELDS, rows, LANES), jnp.float32),
            edge_shape,
            edge_shape,
            pltpu.VMEM((rows, LANES), jnp.float32),
            pltpu.VMEM((BLOCK * TILE, 3 * STEPS * TILE), jnp.bfloat16),
            pltpu.VMEM((TILE, LANES), jnp.int32),
            token_shape,
        ],
        in_specs=[hbm, hbm, vmem(), hbm, hbm],
        out_specs=[vmem()] * 7,
        scratch_shapes=[
            pltpu.SMEM((BLOCKS,), jnp.int32),
            pltpu.SMEM((BLOCKS,), jnp.int32),
            pltpu.VMEM((cm, K, FIELDS, rows, LANES), jnp.bfloat16),
            pltpu.VMEM((rows, LANES), jnp.float32),
            pltpu.SemaphoreType.DMA((3 + len(LOADS),)),
        ],
        compiler_params=SMALL,
        name="synthesis",
    )(far(block_order), far(block_flips), near(small), far(hat), far(mean_speed))

    peers = lax.axis_size("blk")
    from_chip = lax.ppermute(chip_edge, "blk", [(i, i ^ 1) for i in range(peers)])
    joints = [(i, i + 1) for i in range(1, peers - 1, 2)]
    from_far = lax.ppermute(far_edge, "blk", joints + [(j, i) for i, j in joints])

    keep, send, arrived = [None] * 3, [None] * 3, [None] * 3
    for k in range(K):
        kernel = functools.partial(inner_kernel, k, masks_of[k][0])
        shape = pltpu.VMEM((STEPS, FIELDS, half, LANES), jnp.float32)
        keep[k], send[k], token = call(kernel, f"inner{k}", [shape] * 2, forcing, speed, token=token)
        arrived[k] = swap(send[k], masks_of[k][0])

    def edges():
        nonlocal token
        kernel = functools.partial(edge_kernel, masks_of[2][0])
        shape = pltpu.VMEM((STEPS, K * FIELDS, TILE, LANES), jnp.float32)
        args = (forcing, speed, from_chip, from_far)
        keep[2], send[2], token = call(kernel, "edges", [shape] * 2, *args, token=token)
        arrived[2] = swap(send[2], masks_of[2][0])

    whole = [None] * 3
    other = [None] * 3

    def fold(i):
        nonlocal token
        x = keep[i]
        shape = pltpu.VMEM((x.shape[0] // 2,) + x.shape[1:], x.dtype)
        kernel = functools.partial(fold_kernel, masks_of[i][1])
        keep[i], send[i], token = call(kernel, f"fold{i}", [shape] * 2, x, arrived[i], token=token)
        arrived[i] = swap(send[i], masks_of[i][1])

    def add(i, masks):
        nonlocal token
        x = keep[i]
        keep[i], token = call(add_kernel, f"add{i}", [pltpu.VMEM(x.shape, x.dtype)], x, arrived[i], token=token)
        arrived[i] = swap(keep[i], masks)

    def join(i):
        nonlocal token
        x = keep[i]
        shape = pltpu.VMEM((x.shape[0] * 2,) + x.shape[1:], x.dtype)
        kernel = functools.partial(join_kernel, masks_of[i][1])
        whole[i], token = call(kernel, f"join{i}", [shape], x, arrived[i], token=token)
        other[i] = swap(whole[i], masks_of[i][0])

    out = None
    total_tiles = rows // TILE

    def analyse(i, x, is_other):
        nonlocal out, token
        units, tiles = x.shape[1], x.shape[2] // TILE
        extra = [] if out is None else [out]

        def first_tile():
            bit = bit_at(masks_of[i][0])
            bit = 1 - bit if is_other else bit
            return 1 + bit * (half // TILE) if i < K else bit * (total_tiles - 1)

        out, token = pl.pallas_call(
            functools.partial(analysis_kernel, first_tile, i * FIELDS if i < K else 0),
            out_shape=[
                jax.ShapeDtypeStruct((cm, K * FIELDS, total_tiles, TILE, LANES), jnp.float32),
                token_shape,
            ],
            in_specs=[vmem()] * 3 + [pl.BlockSpec(memory_space=pl.ANY)] + [hbm] * len(extra),
            out_specs=[hbm, vmem()],
            scratch_shapes=[
                pltpu.VMEM((tiles, cm, units, TILE, LANES), jnp.float32),
                pltpu.SemaphoreType.DMA((tiles * units // FIELDS,)),
            ],
            input_output_aliases={4: 0} if extra else {},
            compiler_params=SMALL,
            name=f"analysis{i}",
        )(near(meta), near(table), near(x), token, *extra)

    fold(0)
    edges()
    fold(1)
    add(0, masks_of[0][2])
    add(1, masks_of[1][2])
    fold(2)
    add(0, masks_of[0][1])
    add(1, masks_of[1][1])
    add(2, masks_of[2][2])
    join(0)
    join(1)
    add(2, masks_of[2][1])
    analyse(0, whole[0], False)
    analyse(1, whole[1], False)
    join(2)
    analyse(0, other[0], True)
    analyse(2, whole[2], False)
    analyse(1, other[1], True)
    analyse(2, other[2], True)
    return out.reshape(2, freq_local, K, FIELDS, rows, LANES)


def solution(mesh):
    placed = (P(None, "freq", None, None, "blk", None), P("blk", None), P("blk"), P("blk"))
    return jax.shard_map(
        local,
        mesh=mesh,
        in_specs=placed,
        out_specs=P(None, "freq", None, None, "blk", None),
        check_vma=False,
    )
```
